256 devices in a mesh: seq: 32 (over x, y, core), tensor: 8 (over z).
Axes of the slice: x: 4, y: 4, z: 8, core: 2. Of those that a mesh axis runs over, the one named last changes fastest.
Arguments:
- weight: bfloat16 [131072, 5376], P(('seq', 'tensor')), may hold values from -2.2 to 2.2
- hidden: bfloat16 [256, 5376], P('seq'), may hold values from -3.2 to 3.2
- targets: int32 [256], replicated, may hold values from 0 to 131071
- branch: int32 [256], replicated, may hold values from 0 to 2
- pair_of_row: int32 [256], replicated, may hold values from 0 to 63, never falling along the last dimension, each value on 1 to 12 neighbouring positions
- ref_log_prob: float32 [256], replicated, may hold values from -20 to -12
- pair_weight: float32 [64], replicated, may hold values from 2 to 16
- token_ids: int32 [51200], P(('seq', 'tensor')), may hold values from 0 to 131071, as said below
- token_grad: bfloat16 [51200, 5376], P(('seq', 'tensor')), may hold values from -0.059814453 to 0.059814453
Outputs:
- dpo_loss: float32 [], replicated
- weight_grad: bfloat16 [131072, 5376], P(('seq', 'tensor'))
- hidden_grad: bfloat16 [256, 5376], P('seq')
The draws below stay inside these ranges and needn't reach their ends.
Inputs may be any that keep to these rules, and one draw needn't show every extreme that they name: `token_ids`: ids of one device's 200 rows fall at most 2 times into the 512 vocabulary rows of any one device; in every draw one such block of vocabulary rows receives exactly 2 ids from every device.
All inputs are finite; a program needn't handle non-finite values.
Results may differ from the reference program's by a relative error of at most 0.007.
Values may be sent and summed in bfloat16 or wider, within the bound.
No kernel may reach another device: no remote copies, remote signals or barrier semaphores. Data moves between devices by JAX's collectives and lax.ppermute only.
A program may use at most 128 MiB of HBM per device.

```python
import math
import jax
import jax.numpy as jnp
import numpy as np
from jax import lax

D = 5376
VOCAB_DEV = 512
VOCAB = 131072
RESP = 256
PAIRS = 64
PAIR_MOST = 12
TOK_DEV = 200
TOKENS = 51200
CAP = 2
N_TENSOR = 8
DEVICES = 256


def draw_weight(key, part):
    key = jax.random.fold_in(key, 11)
    noise_key = jax.random.fold_in(key, 0)
    sign_key = jax.random.fold_in(key, 2)
    signs = (2 * jax.random.randint(sign_key, (1, D), 0, 2) - 1).astype(jnp.float32)
    shared = 0.3 * signs
    values = 0.2 * jnp.clip(jax.random.normal(noise_key, (VOCAB, D), jnp.float32), -4.5, 4.5)
    values = values + shared
    return values.astype(jnp.bfloat16)


def draw_hidden(key, part):
    key = jax.random.fold_in(key, 12)
    noise_key = jax.random.fold_in(key, 0)
    values = 0.21 * jnp.clip(jax.random.normal(noise_key, (RESP, D), jnp.float32), -4.5, 4.5)
    return values.astype(jnp.bfloat16)


def draw_token_ids(key, part):
    key = jax.random.fold_in(key, 13)
    hot_key, score_key, offset_key = jax.random.split(key, 3)
    slot_count = DEVICES * CAP
    hot_owner = jax.random.randint(hot_key, (), 0, DEVICES)

    def one_block(block_key):
        score_part, shuffle_part = jax.random.split(block_key)
        slot_index = jnp.arange(slot_count, dtype=jnp.int32)
        scores = jax.random.randint(score_part, (slot_count,), 0, 2 ** 19) * 2048 + slot_index
        scores = jnp.where(slot_index // CAP == hot_owner, -1, scores)
        picked_scores, picked = lax.top_k(scores, TOK_DEV - CAP)
        owners = jnp.concatenate([jnp.full((CAP,), hot_owner, jnp.int32), (picked // CAP).astype(jnp.int32)])
        return jax.random.permutation(shuffle_part, owners)
    owners = jax.vmap(one_block)(jax.random.split(score_key, DEVICES)).reshape(TOKENS)
    return owners * VOCAB_DEV + jax.random.randint(offset_key, (TOKENS,), 0, VOCAB_DEV)


def place_ends(entries, rng, low, high):
    shape = entries.shape
    index_at = [jax.random.randint(jax.random.fold_in(rng, axis), (), 0, shape[axis]) for axis in range(len(shape))]
    entries = entries.at[tuple(index_at)].set(low)
    longest = shape.index(max(shape))
    index_at[longest] = (index_at[longest] + 1) % shape[longest]
    return entries.at[tuple(index_at)].set(high)


def steps_of(stream_key, shape, cuts, smallest, high):
    def one(dim, blocks):
        heights = jax.random.uniform(jax.random.fold_in(jax.random.fold_in(stream_key, 6), dim), (blocks,), jnp.float32, smallest / len(cuts), high / len(cuts))
        return jnp.repeat(jnp.exp(heights), shape[dim] // blocks).reshape((-1,) + (1,) * (len(shape) - dim - 1))

    gain = one(*cuts[0])
    for cut in cuts[1:]:
        gain = gain * one(*cut)
    return gain


def length_profile(count, total, limit, skew):
    portions = [(1 << 20) // math.isqrt(grade ** skew) + 1 for grade in range(2, count + 1)]
    spare, given = total - limit - (count - 1), [1] * (count - 1)
    while spare > 0:
        candidates = [i for i in range(count - 1) if given[i] < limit]
        whole, left = sum([portions[i] for i in candidates]), spare
        for i in candidates:
            extra = min(limit - given[i], max(1, left * portions[i] // whole), spare)
            given[i] = given[i] + extra
            spare = spare - extra
    return np.array([limit] + given)


def uneven_parts(rng, number_of, total, most, slope):
    if number_of == 2:
        one = jax.random.randint(rng, (), max(1, total - most), min(most, total - 1) + 1)
        return jnp.stack([one, total - one])
    tallies = jnp.asarray(length_profile(number_of, total, most, slope), jnp.int32)
    pairs = (number_of - 1) // 2
    donor, taker = tallies[1:1 + 2 * pairs:2], tallies[2:2 + 2 * pairs:2]
    slack = jnp.minimum(donor - 1, most - taker)
    shifted = jax.random.randint(jax.random.fold_in(rng, 1), (pairs,), 0, 1 << 20) % (slack + 1)
    tallies = tallies.at[1:1 + 2 * pairs:2].set(donor - shifted).at[2:2 + 2 * pairs:2].set(taker + shifted)
    return tallies[jax.random.permutation(jax.random.fold_in(rng, 2), number_of)]


def centred(stream_key, dims, width, most, pieces=(), held_as=jnp.bfloat16):
    factor_of = steps_of(stream_key, dims, pieces, -0.22, 0.18) if pieces else 1.0
    values = jax.random.normal(stream_key, dims, jnp.float32) * width * factor_of
    return jnp.minimum(jnp.maximum(values, -most), most).astype(held_as)


def setup_inputs(seed: int = 0) -> dict:
    arg_keys = jax.random.split(jax.random.key(seed), 10)
    return {
        "weight": draw_weight(jax.random.fold_in(arg_keys[9], 71), 0),
        "hidden": draw_hidden(jax.random.fold_in(arg_keys[9], 71), 0),
        "targets": place_ends(jax.random.randint(arg_keys[2], (RESP,), 0, VOCAB), jax.random.fold_in(arg_keys[2], 1), 0, VOCAB - 1).astype(jnp.int32),
        "branch": place_ends(jax.random.randint(arg_keys[3], (RESP,), 0, 3), jax.random.fold_in(arg_keys[3], 1), 0, 2).astype(jnp.int32),
        "pair_of_row": jnp.searchsorted(jnp.cumsum(uneven_parts(arg_keys[4], PAIRS, RESP, PAIR_MOST, 1)), jnp.arange(RESP), side="right").astype(jnp.int32),
        "ref_log_prob": jnp.clip(jax.random.uniform(arg_keys[5], (RESP,), jnp.float32, -20.0, -12.0), -20.0, -12.0),
        "pair_weight": jnp.clip(jnp.exp(jax.random.uniform(arg_keys[6], (PAIRS,), jnp.float32, math.log(2.0), math.log(16.0))), 2.0, 16.0),
        "token_ids": draw_token_ids(jax.random.fold_in(arg_keys[9], 71), 0),
        "token_grad": centred(arg_keys[8], (TOKENS, D), 0.01, 0.059814453, ((0, 256),)),
    }


dpo_beta = 0.1

def reference(weight, hidden, targets, branch, pair_of_row, ref_log_prob, pair_weight, token_ids, token_grad):
    vocab_block = VOCAB_DEV * N_TENSOR
    block_count = VOCAB // vocab_block
    logits = jnp.dot(hidden, weight.T, preferred_element_type=jnp.float32)
    row_top = lax.optimization_barrier(jnp.max(logits, axis=1))
    row_total = lax.optimization_barrier(jnp.sum(jnp.exp(logits - row_top[:, None]), axis=1))
    target_logit = jnp.take_along_axis(logits, targets[:, None].astype(jnp.int32), axis=1)[:, 0]
    log_prob = target_logit - row_top - jnp.log(row_total)
    branch_sign = (branch == 1).astype(jnp.float32) - (branch == 2).astype(jnp.float32)
    member = (pair_of_row[:, None] == jnp.arange(PAIRS, dtype=jnp.int32)[None, :]).astype(jnp.float32)
    margin = lax.optimization_barrier(jnp.sum(member * (branch_sign * (log_prob - ref_log_prob))[:, None], axis=0))
    dpo_loss = jnp.sum(pair_weight * jax.nn.softplus(-dpo_beta * margin))
    push_back = pair_weight * jax.nn.sigmoid(-dpo_beta * margin)
    row_scale = -dpo_beta * branch_sign * lax.optimization_barrier(jnp.sum(member * push_back[None, :], axis=1))
    norm_factor = math.sqrt(D)
    grad_float = token_grad.astype(jnp.float32)
    weight_blocks = weight.reshape(block_count, vocab_block, D)
    logit_blocks = logits.reshape(RESP, block_count, vocab_block).transpose(1, 0, 2)
    block_starts = jnp.arange(block_count, dtype=jnp.int32) * vocab_block
    columns = jnp.arange(vocab_block, dtype=jnp.int32)

    def block_grads(carry, stacked):
        weight_rows, block_logits, begin_row = stacked
        target_hit = (columns[None, :] == (targets - begin_row)[:, None]).astype(jnp.float32)
        probs = jnp.exp(block_logits - row_top[:, None]) / row_total[:, None]
        dlogits = (row_scale[:, None] * (target_hit - probs)).astype(jnp.bfloat16)
        head_grad = jnp.dot(dlogits.T, hidden, preferred_element_type=jnp.float32)
        local_ids = token_ids - begin_row
        inside = (local_ids >= 0) & (local_ids < vocab_block)
        landing = jnp.where(inside, local_ids, vocab_block).astype(jnp.int32)
        embed_grad = jax.ops.segment_sum(grad_float, landing, num_segments=vocab_block + 1)[:vocab_block]
        block_out = (head_grad + norm_factor * embed_grad).astype(jnp.bfloat16)
        return (carry + jnp.dot(dlogits, weight_rows, preferred_element_type=jnp.float32), block_out)
    row_sum, grad_blocks = lax.scan(block_grads, jnp.zeros((RESP, D), jnp.float32), (weight_blocks, logit_blocks, block_starts))
    return (dpo_loss, grad_blocks.reshape(VOCAB, D), row_sum.astype(jnp.bfloat16))
```

```python
import math

import jax
import jax.numpy as jnp
from jax import lax
from jax.sharding import Mesh
from jax.sharding import PartitionSpec as P

dpo_beta = 0.1
planes = (("core", 2), ("y", 4), ("x", 4))


def others(value, axis):
    size = lax.axis_size(axis)
    return [
        lax.ppermute(value, axis, [(i, (i + step) % size) for i in range(size)])
        for step in range(1, size)
    ]


def gather_rows(hidden):
    rows = hidden
    for axis in ("x", "y", "core"):
        rows = jnp.concatenate([rows] + others(rows, axis), axis=0)
    return rows


def shards(
    weight, hidden, targets, branch, pair_of_row, ref_log_prob, pair_weight, token_ids, token_grad
):
    vocab_rows, model_width = weight.shape
    owned = hidden.shape[0]
    x, y, core, z = (lax.axis_index(a) for a in ("x", "y", "core", "tensor"))
    nx, ny, nc, nz = (lax.axis_size(a) for a in ("x", "y", "core", "tensor"))
    seq_count = nx * ny * nc
    owners = seq_count * nz
    me = ((x * ny + y) * nc + core) * nz + z
    vocab_start = me * vocab_rows

    token_count = token_ids.shape[0]
    capacity = max(2, (2 * token_count + owners - 1) // owners)
    row_owner = token_ids // vocab_rows
    local = token_ids - row_owner * vocab_rows
    position = jnp.arange(token_count, dtype=jnp.int32)
    earlier = (row_owner[:, None] == row_owner[None, :]) & (position[None, :] < position[:, None])
    slot = jnp.sum(earlier.astype(jnp.int32), axis=1)
    pick = (
        (jnp.arange(owners, dtype=jnp.int32)[:, None, None] == row_owner[None, None, :])
        & (jnp.arange(capacity, dtype=jnp.int32)[None, :, None] == slot[None, None, :])
    ).astype(jnp.bfloat16)
    lane = jnp.arange(128, dtype=jnp.int32)[None, :]
    tag = jnp.where(lane == 0, (local // 256 + 1)[:, None], jnp.where(lane == 1, (local % 256)[:, None], 0))
    tagged = jnp.concatenate([token_grad, tag.astype(jnp.bfloat16)], axis=1)
    outgoing = jnp.einsum("psr,rd->psd", pick, tagged, preferred_element_type=jnp.float32).astype(
        jnp.bfloat16
    )
    arrived = lax.all_to_all(outgoing, ("x", "y", "core", "tensor"), 0, 0, tiled=True)

    gathered = gather_rows(hidden)
    step_c, step_y, step_x = jnp.meshgrid(
        jnp.arange(nc), jnp.arange(ny), jnp.arange(nx), indexing="ij"
    )
    from_x = (x - step_x + nx) % nx
    from_y = (y - step_y + ny) % ny
    from_c = (core - step_c + nc) % nc
    block_of = ((from_x * ny + from_y) * nc + from_c).reshape(-1)
    row_of = (block_of[:, None] * owned + jnp.arange(owned)[None, :]).reshape(-1)

    logits = lax.dot_general(
        gathered, weight, (((1,), (1,)), ((), ())), preferred_element_type=jnp.float32
    )
    place = (row_of[:, None] == jnp.arange(row_of.shape[0])[None, :])
    def take(v):
        return jnp.sum(jnp.where(place, v[None, :], 0), axis=1)
    def untake(v):
        return jnp.sum(jnp.where(place, v[:, None], 0), axis=0)
    my_targets = take(targets)
    columns = jnp.arange(vocab_rows, dtype=jnp.int32)
    target_hit = (columns[None, :] == (my_targets - vocab_start)[:, None]).astype(jnp.float32)
    target_part = jnp.sum(logits * target_hit, axis=1)
    top_part = jnp.max(logits, axis=1)
    total_part = jnp.sum(jnp.exp(logits - top_part[:, None]), axis=1)
    stats = jnp.stack([untake(top_part), untake(total_part), untake(target_part)])
    for axis in ("core", "y", "x", "tensor"):
        both = jnp.stack([stats] + others(stats, axis))
        top = jnp.max(both[:, 0], axis=0)
        total = jnp.sum(both[:, 1] * jnp.exp(both[:, 0] - top[None]), axis=0)
        stats = jnp.stack([top, total, jnp.sum(both[:, 2], axis=0)])
    row_top, row_total, target_logit = stats[0], stats[1], stats[2]
    log_prob = target_logit - row_top - jnp.log(row_total)
    branch_sign = (branch == 1).astype(jnp.float32) - (branch == 2).astype(jnp.float32)
    pair_count = pair_weight.shape[0]
    member = (pair_of_row[:, None] == jnp.arange(pair_count, dtype=jnp.int32)[None, :]).astype(
        jnp.float32
    )
    margin = jnp.sum(member * (branch_sign * (log_prob - ref_log_prob))[:, None], axis=0)
    dpo_loss = jnp.sum(pair_weight * jax.nn.softplus(-dpo_beta * margin))
    push_back = pair_weight * jax.nn.sigmoid(-dpo_beta * margin)
    row_scale = -dpo_beta * branch_sign * jnp.sum(member * push_back[None, :], axis=1)
    probs = jnp.exp(logits - take(row_top)[:, None]) / take(row_total)[:, None]
    dlogits = (take(row_scale)[:, None] * (target_hit - probs)).astype(jnp.bfloat16)

    part = jnp.dot(dlogits, weight, preferred_element_type=jnp.float32)
    for axis in ("core", "y", "x"):
        size = lax.axis_size(axis)
        blocks = part.reshape(size, part.shape[0] // size, model_width)
        sends = blocks.astype(jnp.bfloat16)
        total = blocks[0]
        for step in range(1, size):
            total = total + lax.ppermute(
                sends[step], axis, [(i, (i - step) % size) for i in range(size)]
            ).astype(jnp.float32)
        part = total
    sent = part.astype(jnp.bfloat16)
    hidden_grad = (part + sum(o.astype(jnp.float32) for o in others(sent, "tensor"))).astype(jnp.bfloat16)

    head_grad = lax.dot_general(
        dlogits, gathered, (((0,), (0,)), ((), ())), preferred_element_type=jnp.float32
    )
    tags = arrived[:, :, model_width : model_width + 2].astype(jnp.int32)
    ids = (tags[:, :, 0] - 1) * 256 + tags[:, :, 1]
    onehot = (columns[:, None, None] == ids[None]).astype(jnp.bfloat16)
    embed_grad = jnp.einsum(
        "vps,psd->vd", onehot, arrived[:, :, :model_width], preferred_element_type=jnp.float32
    )
    weight_grad = (head_grad + math.sqrt(model_width) * embed_grad).astype(jnp.bfloat16)
    return (dpo_loss, weight_grad, hidden_grad)


def solution(mesh):
    fine = Mesh(mesh.devices.reshape(4, 4, 2, 8), ("x", "y", "core", "tensor"))
    seq = ("x", "y", "core")
    every = ("x", "y", "core", "tensor")
    return jax.shard_map(
        shards,
        mesh=fine,
        in_specs=(P(every, None), P(seq, None), P(), P(), P(), P(), P(), P(every), P(every, None)),
        out_specs=(P(), P(every, None), P(seq, None)),
        check_vma=False,
    )
```

```python
import math

import jax
import jax.numpy as jnp
from jax import lax
from jax.experimental import pallas as pl
from jax.experimental.pallas import tpu as pltpu
from jax.sharding import Mesh
from jax.sharding import PartitionSpec as P

dpo_beta = 0.1


def shift(value, axis, step):
    size = lax.axis_size(axis)
    return lax.ppermute(value, axis, [(i, (i + step) % size) for i in range(size)])


def others(value, axis):
    return [shift(value, axis, step) for step in range(1, lax.axis_size(axis))]


def round_ring(value, axis):
    size = lax.axis_size(axis)
    ahead = behind = value
    found = []
    for step in range(1, size // 2 + 1):
        ahead = shift(ahead, axis, 1)
        found.append(ahead)
        if step < size - step:
            behind = shift(behind, axis, size - 1)
            found.append(behind)
    return found


light = pl.CostEstimate(flops=0, bytes_accessed=0, transcendentals=0)


def spread_call(matrix, rows, depth):
    places, count = matrix.shape
    width = rows.shape[1]
    tile = max(t for t in range(128, 769, 128) if width % t == 0)

    def body(matrix_ref, rows_ref, out_ref):
        found = jnp.dot(matrix_ref[...], rows_ref[...], preferred_element_type=jnp.float32)
        out_ref[...] = found.reshape(places // depth, depth, tile).astype(out_ref.dtype)

    return pl.pallas_call(
        body,
        grid=(width // tile,),
        in_specs=[
            pl.BlockSpec((places, count), lambda j: (0, 0)),
            pl.BlockSpec((count, tile), lambda j: (0, j)),
        ],
        out_specs=pl.BlockSpec((places // depth, depth, tile), lambda j: (0, 0, j)),
        out_shape=jax.ShapeDtypeStruct((places // depth, depth, width), jnp.bfloat16),
        compiler_params=pltpu.CompilerParams(vmem_limit_bytes=48 << 20),
        cost_estimate=light,
    )(matrix, rows)


def product_call(left, weight, pieces):
    rows, depth = left.shape
    width = weight.shape[1]
    tile = max(t for t in range(128, 769, 128) if width % t == 0)
    size = rows // pieces

    def body(left_ref, weight_ref, *outs):
        found = jnp.dot(left_ref[...], weight_ref[...], preferred_element_type=jnp.float32)
        for k, out in enumerate(outs):
            out[...] = found[k * size : (k + 1) * size]

    return pl.pallas_call(
        body,
        grid=(width // tile,),
        in_specs=[
            pl.BlockSpec((rows, depth), lambda j: (0, 0)),
            pl.BlockSpec((depth, tile), lambda j: (0, j)),
        ],
        out_specs=[pl.BlockSpec((size, tile), lambda j: (0, j))] * pieces,
        out_shape=[jax.ShapeDtypeStruct((size, width), jnp.float32)] * pieces,
        compiler_params=pltpu.CompilerParams(vmem_limit_bytes=48 << 20),
        cost_estimate=light,
    )(left, weight)


def sum_call(values, pieces, types):
    rows, width = values[0].shape
    tile = max(t for t in range(128, 1793, 128) if width % t == 0)
    size = rows // pieces

    def body(*refs):
        total = refs[0][...]
        for one in refs[1 : len(values)]:
            total = total + one[...].astype(jnp.float32)
        for k, out in enumerate(refs[len(values) :]):
            out[...] = total[k % pieces * size : (k % pieces + 1) * size].astype(out.dtype)

    return pl.pallas_call(
        body,
        grid=(width // tile,),
        in_specs=[pl.BlockSpec((rows, tile), lambda j: (0, j))] * len(values),
        out_specs=[pl.BlockSpec((size, tile), lambda j: (0, j))] * len(types),
        out_shape=[jax.ShapeDtypeStruct((size, width), t) for t in types],
        compiler_params=pltpu.CompilerParams(vmem_limit_bytes=48 << 20),
        cost_estimate=light,
    )(*values)


def shards(
    weight, hidden, targets, branch, pair_of_row, ref_log_prob, pair_weight, token_ids, token_grad
):
    vocab_rows, model_width = weight.shape
    owned = hidden.shape[0]
    x, y, core, z = (lax.axis_index(a) for a in ("x", "y", "core", "tensor"))
    nx, ny, nc, nz = (lax.axis_size(a) for a in ("x", "y", "core", "tensor"))
    owners = nx * ny * nc * nz
    me = ((x * ny + y) * nc + core) * nz + z
    vocab_start = me * vocab_rows
    every = ("x", "y", "core", "tensor")

    token_count = token_ids.shape[0]
    capacity = max(2, (2 * token_count + owners - 1) // owners)
    row_owner = token_ids // vocab_rows
    local = token_ids - row_owner * vocab_rows
    position = jnp.arange(token_count, dtype=jnp.int32)
    earlier = (row_owner[:, None] == row_owner[None, :]) & (position[None, :] < position[:, None])
    slot = jnp.sum(earlier.astype(jnp.int32), axis=1)
    pick = (
        jnp.arange(owners * capacity, dtype=jnp.int32)[:, None]
        == (row_owner * capacity + slot)[None, :]
    ).astype(jnp.bfloat16)
    lane = jnp.arange(128, dtype=jnp.int32)[None, :]
    tag = jnp.where(
        lane == 0, (local // 256 + 1)[:, None], jnp.where(lane == 1, (local % 256)[:, None], 0)
    )
    half = model_width // 256 * 128
    first_part = jnp.concatenate([token_grad[:, :half], tag.astype(jnp.bfloat16)], axis=1)
    second_part = token_grad[:, half:]

    out_first = spread_call(pick, first_part, capacity)
    out_second = spread_call(pick, second_part, capacity)
    arrived_first = lax.all_to_all(out_first, every, 0, 0, tiled=True)

    rows = hidden
    for axis in ("x", "y"):
        rows = jnp.concatenate([rows] + others(rows, axis), axis=0)
    gathered = jnp.concatenate([rows, shift(rows, "core", 1)], axis=0)
    step_y, step_x = jnp.meshgrid(jnp.arange(ny), jnp.arange(nx), indexing="ij")
    plane = ((x - step_x + nx) % nx * ny + (y - step_y + ny) % ny).reshape(-1)
    block_of = jnp.concatenate([plane * nc + core, plane * nc + (core + 1) % nc])
    row_of = (block_of[:, None] * owned + jnp.arange(owned)[None, :]).reshape(-1)

    logits = lax.dot_general(
        gathered, weight, (((1,), (1,)), ((), ())), preferred_element_type=jnp.float32
    )
    place = row_of[:, None] == jnp.arange(row_of.shape[0])[None, :]

    def take(v):
        return jnp.sum(jnp.where(place, v[None, :], 0), axis=1)

    def untake(v):
        return jnp.sum(jnp.where(place, v[:, None], 0), axis=0)

    columns = jnp.arange(vocab_rows, dtype=jnp.int32)
    target_hit = (columns[None, :] == (take(targets) - vocab_start)[:, None]).astype(jnp.float32)
    target_part = jnp.sum(logits * target_hit, axis=1)
    top_part = jnp.max(logits, axis=1)
    total_part = jnp.sum(jnp.exp(logits - top_part[:, None]), axis=1)
    stats = jnp.stack([untake(top_part), untake(total_part), untake(target_part)])
    def merge(both):
        top = both[0][0]
        for one in both[1:]:
            top = jnp.maximum(top, one[0])
        total = sum(one[1] * jnp.exp(one[0] - top) for one in both)
        return jnp.stack([top, total, sum(one[2] for one in both)])

    for axis in ("core", "y", "x"):
        stats = merge([stats] + others(stats, axis))
    stats, arrived_first, out_second = lax.optimization_barrier((stats, arrived_first, out_second))
    for step in (1, 2, 4):
        stats = merge([stats, shift(stats, "tensor", step)])
    stats, out_second = lax.optimization_barrier((stats, out_second))
    arrived_second = lax.all_to_all(out_second, every, 0, 0, tiled=True)
    row_top, row_total, target_logit = stats[0], stats[1], stats[2]
    log_prob = target_logit - row_top - jnp.log(row_total)
    branch_sign = (branch == 1).astype(jnp.float32) - (branch == 2).astype(jnp.float32)
    pair_count = pair_weight.shape[0]
    member = (pair_of_row[:, None] == jnp.arange(pair_count, dtype=jnp.int32)[None, :]).astype(
        jnp.float32
    )
    margin = jnp.sum(member * (branch_sign * (log_prob - ref_log_prob))[:, None], axis=0)
    dpo_loss = jnp.sum(pair_weight * jax.nn.softplus(-dpo_beta * margin))
    push_back = pair_weight * jax.nn.sigmoid(-dpo_beta * margin)
    row_scale = -dpo_beta * branch_sign * jnp.sum(member * push_back[None, :], axis=1)
    probs = jnp.exp(logits - take(row_top)[:, None]) / take(row_total)[:, None]
    dlogits = (take(row_scale)[:, None] * (target_hit - probs)).astype(jnp.bfloat16)

    narrow, wide = jnp.bfloat16, jnp.float32
    pieces = product_call(dlogits, weight, nc)
    for axis, types in (
        ("core", [wide] + [narrow] * (ny - 1)),
        ("y", [wide] * nx),
        ("x", [wide, narrow]),
    ):
        size = lax.axis_size(axis)
        came = [shift(pieces[step], axis, size - step) for step in range(1, size)]
        pieces = sum_call([pieces[0]] + came, 1 if axis == "x" else len(types), types)
    part, sent = pieces
    head_grad = lax.dot_general(
        dlogits, gathered, (((0,), (0,)), ((), ())), preferred_element_type=jnp.float32
    )
    tags = arrived_first[:, :, half : half + 2].astype(jnp.int32)
    ids = (tags[:, :, 0] - 1) * 256 + tags[:, :, 1]
    onehot = (columns[:, None, None] == ids[None]).astype(jnp.bfloat16)

    def collect(arrived, head):
        embed = jnp.einsum("vps,psd->vd", onehot, arrived, preferred_element_type=jnp.float32)
        return (head + math.sqrt(model_width) * embed).astype(jnp.bfloat16)

    first_grad = collect(arrived_first[:, :, :half], head_grad[:, :half])
    second_head = head_grad[:, half:]
    sent, first_grad, second_head, arrived_second = lax.optimization_barrier(
        (sent, first_grad, second_head, arrived_second)
    )
    hidden_grad = part + sum(o.astype(jnp.float32) for o in round_ring(sent, "tensor"))
    hidden_grad = hidden_grad.astype(jnp.bfloat16)

    weight_grad = jnp.concatenate([first_grad, collect(arrived_second, second_head)], axis=1)
    return (dpo_loss, weight_grad, hidden_grad)


def solution(mesh):
    fine = Mesh(mesh.devices.reshape(4, 4, 2, 8), ("x", "y", "core", "tensor"))
    seq = ("x", "y", "core")
    every = ("x", "y", "core", "tensor")
    return jax.shard_map(
        shards,
        mesh=fine,
        in_specs=(P(every, None), P(seq, None), P(), P(), P(), P(), P(), P(every), P(every, None)),
        out_specs=(P(), P(every, None), P(seq, None)),
        check_vma=False,
    )
```

```python
import math

import jax
import jax.numpy as jnp
from jax import lax
from jax.experimental import pallas as pl
from jax.experimental.pallas import tpu as pltpu
from jax.sharding import Mesh
from jax.sharding import PartitionSpec as P

dpo_beta = 0.1


def shift(value, axis, step):
    size = lax.axis_size(axis)
    return lax.ppermute(value, axis, [(i, (i + step) % size) for i in range(size)])


def others(value, axis):
    return [shift(value, axis, step) for step in range(1, lax.axis_size(axis))]


def round_ring(value, axis):
    size = lax.axis_size(axis)
    ahead = behind = value
    found = []
    for step in range(1, size // 2 + 1):
        ahead = shift(ahead, axis, 1)
        found.append(ahead)
        if step < size - step:
            behind = shift(behind, axis, size - 1)
            found.append(behind)
    return found


light = pl.CostEstimate(flops=0, bytes_accessed=0, transcendentals=0)


def spread_call(matrix, rows, depth):
    places, count = matrix.shape
    width = rows.shape[1]
    tile = max(t for t in range(128, 769, 128) if width % t == 0)

    def body(matrix_ref, rows_ref, out_ref):
        found = jnp.dot(matrix_ref[...], rows_ref[...], preferred_element_type=jnp.float32)
        out_ref[...] = found.reshape(places // depth, depth, tile).astype(out_ref.dtype)

    return pl.pallas_call(
        body,
        grid=(width // tile,),
        in_specs=[
            pl.BlockSpec((places, count), lambda j: (0, 0)),
            pl.BlockSpec((count, tile), lambda j: (0, j)),
        ],
        out_specs=pl.BlockSpec((places // depth, depth, tile), lambda j: (0, 0, j)),
        out_shape=jax.ShapeDtypeStruct((places // depth, depth, width), jnp.bfloat16),
        compiler_params=pltpu.CompilerParams(vmem_limit_bytes=48 << 20),
        cost_estimate=light,
    )(matrix, rows)


def product_call(left, weight, pieces):
    rows, depth = left.shape
    width = weight.shape[1]
    tile = max(t for t in range(128, 1793, 128) if width % t == 0)
    size = rows // pieces

    def body(left_ref, weight_ref, *outs):
        found = jnp.dot(left_ref[...], weight_ref[...], preferred_element_type=jnp.float32)
        for k, out in enumerate(outs):
            out[...] = found[k * size : (k + 1) * size]

    return pl.pallas_call(
        body,
        grid=(width // tile,),
        in_specs=[
            pl.BlockSpec((rows, depth), lambda j: (0, 0)),
            pl.BlockSpec((depth, tile), lambda j: (0, j)),
        ],
        out_specs=[pl.BlockSpec((size, tile), lambda j: (0, j))] * pieces,
        out_shape=[jax.ShapeDtypeStruct((size, width), jnp.float32)] * pieces,
        compiler_params=pltpu.CompilerParams(vmem_limit_bytes=48 << 20),
        cost_estimate=light,
    )(left, weight)


def sum_call(values, group, picks, types, begin=0, width=None):
    rows, full = values[0].shape
    width = full if width is None else width
    tile = max(t for t in range(128, 1793, 128) if width % t == 0 and begin % t == 0)

    def body(*refs):
        total = refs[0][...]
        for one in refs[1 : len(values)]:
            total = total + one[...].astype(jnp.float32)
        for pick, out in zip(picks, refs[len(values) :]):
            held = [total[g * group : (g + 1) * group] for g in pick]
            held = held[0] if len(held) == 1 else jnp.concatenate(held, axis=0)
            out[...] = held.astype(out.dtype)

    return pl.pallas_call(
        body,
        grid=(width // tile,),
        in_specs=[pl.BlockSpec((rows, tile), lambda j: (0, j + begin // tile))] * len(values),
        out_specs=[pl.BlockSpec((group * len(pick), tile), lambda j: (0, j)) for pick in picks],
        out_shape=[
            jax.ShapeDtypeStruct((group * len(pick), width), t) for pick, t in zip(picks, types)
        ],
        compiler_params=pltpu.CompilerParams(vmem_limit_bytes=48 << 20),
        cost_estimate=light,
    )(*values)


def join_call(parts):
    heights = [one.shape[0] for one in parts]
    width = parts[0].shape[1]
    tile = max(t for t in range(128, 2689, 128) if width % t == 0)

    def body(*refs):
        held = [one[...].astype(jnp.float32) for one in refs[:-1]]
        refs[-1][...] = jnp.concatenate(held, axis=0).astype(refs[-1].dtype)

    return pl.pallas_call(
        body,
        grid=(width // tile,),
        in_specs=[pl.BlockSpec((h, tile), lambda j: (0, j)) for h in heights],
        out_specs=pl.BlockSpec((sum(heights), tile), lambda j: (0, j)),
        out_shape=jax.ShapeDtypeStruct((sum(heights), width), parts[0].dtype),
        compiler_params=pltpu.CompilerParams(vmem_limit_bytes=48 << 20),
        cost_estimate=light,
    )(*parts)


def logits_call(parts, weight):
    height = parts[0].shape[0]
    slab, width = weight.shape
    tile = max(t for t in range(128, 1793, 128) if width % t == 0)

    def body(*refs):
        *ins, weight_ref, out = refs

        @pl.when(pl.program_id(0) == 0)
        def _():
            out[...] = jnp.zeros_like(out)

        for k, one in enumerate(ins):
            out[k * height : (k + 1) * height, :] += lax.dot_general(
                one[...], weight_ref[...], (((1,), (1,)), ((), ())),
                preferred_element_type=jnp.float32,
            )

    return pl.pallas_call(
        body,
        grid=(width // tile,),
        in_specs=[pl.BlockSpec((height, tile), lambda j: (0, j))] * len(parts)
        + [pl.BlockSpec((slab, tile), lambda j: (0, j))],
        out_specs=pl.BlockSpec((height * len(parts), slab), lambda j: (0, 0)),
        out_shape=jax.ShapeDtypeStruct((height * len(parts), slab), jnp.float32),
        compiler_params=pltpu.CompilerParams(vmem_limit_bytes=48 << 20),
        cost_estimate=light,
    )(*parts, weight)


def finish_call(turned, rows, hot, arrived, tile, begin, count, begun=None):
    width = rows.shape[1]
    slab, slots = hot.shape
    owners, depth, _ = arrived.shape
    scale = math.sqrt(width)

    def body(turned_ref, rows_ref, hot_ref, arrived_ref, *rest):
        head = jnp.dot(turned_ref[...], rows_ref[...], preferred_element_type=jnp.float32)
        flat = arrived_ref[...].astype(jnp.float32).reshape(slots, tile).astype(jnp.bfloat16)
        embed = jnp.dot(hot_ref[...], flat, preferred_element_type=jnp.float32)
        rest[-1][...] = (head + scale * embed).astype(jnp.bfloat16)

    more = [] if begun is None else [begun]
    return pl.pallas_call(
        body,
        grid=(count,),
        in_specs=[
            pl.BlockSpec(turned.shape, lambda j: (0, 0)),
            pl.BlockSpec((rows.shape[0], tile), lambda j: (0, j + begin)),
            pl.BlockSpec(hot.shape, lambda j: (0, 0)),
            pl.BlockSpec((owners, depth, tile), lambda j: (0, 0, j)),
        ]
        + [pl.BlockSpec(memory_space=pl.ANY)] * len(more),
        out_specs=pl.BlockSpec((slab, tile), lambda j: (0, j + begin)),
        out_shape=jax.ShapeDtypeStruct((slab, width), jnp.bfloat16),
        input_output_aliases={4: 0} if more else {},
        compiler_params=pltpu.CompilerParams(vmem_limit_bytes=48 << 20),
        cost_estimate=light,
    )(turned, rows, hot, arrived, *more)


def shards(
    weight, hidden, targets, branch, pair_of_row, ref_log_prob, pair_weight, token_ids, token_grad
):
    vocab_rows, model_width = weight.shape
    owned = hidden.shape[0]
    x, y, core, z = (lax.axis_index(a) for a in ("x", "y", "core", "tensor"))
    nx, ny, nc, nz = (lax.axis_size(a) for a in ("x", "y", "core", "tensor"))
    owners = nx * ny * nc * nz
    me = ((x * ny + y) * nc + core) * nz + z
    vocab_start = me * vocab_rows
    every = ("x", "y", "core", "tensor")

    token_count = token_ids.shape[0]
    capacity = max(2, (2 * token_count + owners - 1) // owners)
    row_owner = token_ids // vocab_rows
    local = token_ids - row_owner * vocab_rows
    position = jnp.arange(token_count, dtype=jnp.int32)
    earlier = (row_owner[:, None] == row_owner[None, :]) & (position[None, :] < position[:, None])
    slot = jnp.sum(earlier.astype(jnp.int32), axis=1)
    pick = (
        jnp.arange(owners * capacity, dtype=jnp.int32)[:, None]
        == (row_owner * capacity + slot)[None, :]
    ).astype(jnp.bfloat16)
    lane = jnp.arange(128, dtype=jnp.int32)[None, :]
    tag = jnp.where(
        lane == 0, (local // 256 + 1)[:, None], jnp.where(lane == 1, (local % 256)[:, None], 0)
    )
    half = model_width // 7 // 128 * 4 * 128
    first_part = jnp.concatenate([token_grad[:, :half], tag.astype(jnp.bfloat16)], axis=1)
    second_part = token_grad[:, half:]

    out_first = spread_call(pick, first_part, capacity)
    out_second = spread_call(pick, second_part, capacity)
    rows = join_call([hidden] + others(hidden, "x"))
    rows, out_first = lax.optimization_barrier((rows, out_first))
    arrived_first = lax.all_to_all(out_first, every, 0, 0, tiled=True)
    came = others(rows, "y")
    *came, out_second = lax.optimization_barrier((*came, out_second))
    rows = join_call([rows] + came)
    halves = [rows, shift(rows, "core", 1)]
    gathered = jnp.concatenate(halves, axis=0)
    step_y, step_x = jnp.meshgrid(jnp.arange(ny), jnp.arange(nx), indexing="ij")
    plane = ((x - step_x + nx) % nx * ny + (y - step_y + ny) % ny).reshape(-1)
    block_of = jnp.concatenate([plane * nc + core, plane * nc + (core + 1) % nc])
    row_of = (block_of[:, None] * owned + jnp.arange(owned)[None, :]).reshape(-1)

    logits = logits_call(halves, weight)
    place = row_of[:, None] == jnp.arange(row_of.shape[0])[None, :]

    def take(v):
        return jnp.sum(jnp.where(place, v[None, :], 0), axis=1)

    def untake(v):
        return jnp.sum(jnp.where(place, v[:, None], 0), axis=0)

    columns = jnp.arange(vocab_rows, dtype=jnp.int32)
    target_hit = (columns[None, :] == (take(targets) - vocab_start)[:, None]).astype(jnp.float32)
    target_part = jnp.sum(logits * target_hit, axis=1)
    top_part = jnp.max(logits, axis=1)
    total_part = jnp.sum(jnp.exp(logits - top_part[:, None]), axis=1)
    stats = jnp.stack([untake(top_part), untake(total_part), untake(target_part)])
    def merge(both):
        top = both[0][0]
        for one in both[1:]:
            top = jnp.maximum(top, one[0])
        total = sum(one[1] * jnp.exp(one[0] - top) for one in both)
        return jnp.stack([top, total, sum(one[2] for one in both)])

    for axis in ("core", "y", "x"):
        stats = merge([stats] + others(stats, axis))
    for step in (1, 2, 4):
        stats = merge([stats, shift(stats, "tensor", step)])
    stats, arrived_first, out_second = lax.optimization_barrier((stats, arrived_first, out_second))
    arrived_second = lax.all_to_all(out_second, every, 0, 0, tiled=True)
    row_top, row_total, target_logit = stats[0], stats[1], stats[2]
    log_prob = target_logit - row_top - jnp.log(row_total)
    branch_sign = (branch == 1).astype(jnp.float32) - (branch == 2).astype(jnp.float32)
    pair_count = pair_weight.shape[0]
    member = (pair_of_row[:, None] == jnp.arange(pair_count, dtype=jnp.int32)[None, :]).astype(
        jnp.float32
    )
    margin = jnp.sum(member * (branch_sign * (log_prob - ref_log_prob))[:, None], axis=0)
    dpo_loss = jnp.sum(pair_weight * jax.nn.softplus(-dpo_beta * margin))
    push_back = pair_weight * jax.nn.sigmoid(-dpo_beta * margin)
    row_scale = -dpo_beta * branch_sign * jnp.sum(member * push_back[None, :], axis=1)
    probs = jnp.exp(logits - take(row_top)[:, None]) / take(row_total)[:, None]
    dlogits = (take(row_scale)[:, None] * (target_hit - probs)).astype(jnp.bfloat16)

    narrow, wide = jnp.bfloat16, jnp.float32
    own, away = product_call(dlogits, weight, nc)
    both = [own, shift(away, "core", nc - 1)]
    columns_each = model_width // 2

    def reduce_along(values, axis, group, picks, types):
        size = lax.axis_size(axis)
        came = [shift(values[step], axis, size - step) for step in range(1, size)]
        return sum_call([values[0]] + came, group, picks, types)

    by_y = [[i * nx + j for j in range(nx)] for i in range(ny)]
    by_x = [[i * nx + j for i in range(ny)] for j in range(nx)]
    side_y = sum_call(both, owned, by_y, [wide] + [narrow] * (ny - 1), 0, columns_each)
    side_x = sum_call(both, owned, by_x, [wide] + [narrow] * (nx - 1), columns_each, columns_each)
    side_y = reduce_along(side_y, "y", owned, [[j] for j in range(nx)], [wide] * nx)
    side_x = reduce_along(side_x, "x", owned, [[i] for i in range(ny)], [wide] * ny)
    side_y = reduce_along(side_y, "x", owned, [[0]], [wide])[0]
    side_x = reduce_along(side_x, "y", owned, [[0]], [wide])[0]
    part = jnp.concatenate([side_y, side_x], axis=1)
    sent = part.astype(narrow)

    tags = arrived_first[:, :, half : half + 2].astype(jnp.int32)
    ids = (tags[:, :, 0] - 1) * 256 + tags[:, :, 1]
    onehot = (columns[:, None] == ids.reshape(-1)[None, :]).astype(jnp.bfloat16)
    turned = dlogits.T
    tile = max(
        t for t in range(128, 769, 128) if half % t == 0 and (model_width - half) % t == 0
    )
    begun = finish_call(turned, gathered, onehot, arrived_first, tile, 0, half // tile)
    sent, begun, arrived_second = lax.optimization_barrier((sent, begun, arrived_second))
    hidden_grad = part + sum(o.astype(jnp.float32) for o in round_ring(sent, "tensor"))
    hidden_grad = hidden_grad.astype(jnp.bfloat16)

    weight_grad = finish_call(
        turned, gathered, onehot, arrived_second, tile, half // tile,
        (model_width - half) // tile, begun,
    )
    return (dpo_loss, weight_grad, hidden_grad)


def solution(mesh):
    fine = Mesh(mesh.devices.reshape(4, 4, 2, 8), ("x", "y", "core", "tensor"))
    seq = ("x", "y", "core")
    every = ("x", "y", "core", "tensor")
    return jax.shard_map(
        shards,
        mesh=fine,
        in_specs=(P(every, None), P(seq, None), P(), P(), P(), P(), P(), P(every), P(every, None)),
        out_specs=(P(), P(every, None), P(seq, None)),
        check_vma=False,
    )
```

```python
import math

import jax
import jax.numpy as jnp
from jax import lax
from jax.experimental import pallas as pl
from jax.experimental.pallas import tpu as pltpu
from jax.sharding import Mesh
from jax.sharding import PartitionSpec as P

dpo_beta = 0.1


def shift(value, axis, step):
    size = lax.axis_size(axis)
    return lax.ppermute(value, axis, [(i, (i + step) % size) for i in range(size)])


def others(value, axis):
    return [shift(value, axis, step) for step in range(1, lax.axis_size(axis))]


def round_ring(near, axis):
    size = lax.axis_size(axis)
    ahead, behind = near
    found = [ahead, behind]
    for step in range(2, size // 2 + 1):
        ahead = shift(ahead, axis, 1)
        found.append(ahead)
        if step < size - step:
            behind = shift(behind, axis, size - 1)
            found.append(behind)
    return found


light = pl.CostEstimate(flops=0, bytes_accessed=0, transcendentals=0)


def spread_call(matrix, rows, depth):
    places, count = matrix.shape
    width = rows.shape[1]
    tile = max(t for t in range(128, 1409, 128) if width % t == 0)

    def body(matrix_ref, rows_ref, out_ref):
        found = jnp.dot(matrix_ref[...], rows_ref[...], preferred_element_type=jnp.float32)
        out_ref[...] = found.reshape(places // depth, depth, tile).astype(out_ref.dtype)

    return pl.pallas_call(
        body,
        grid=(width // tile,),
        in_specs=[
            pl.BlockSpec((places, count), lambda j: (0, 0)),
            pl.BlockSpec((count, tile), lambda j: (0, j)),
        ],
        out_specs=pl.BlockSpec((places // depth, depth, tile), lambda j: (0, 0, j)),
        out_shape=jax.ShapeDtypeStruct((places // depth, depth, width), jnp.bfloat16),
        compiler_params=pltpu.CompilerParams(vmem_limit_bytes=48 << 20),
        cost_estimate=light,
    )(matrix, rows)


def product_call(left, weight, pieces):
    rows, depth = left.shape
    width = weight.shape[1]
    tile = max(t for t in range(128, 1793, 128) if width % t == 0)
    size = rows // pieces

    def body(left_ref, weight_ref, *outs):
        found = jnp.dot(left_ref[...], weight_ref[...], preferred_element_type=jnp.float32)
        for k, out in enumerate(outs):
            out[...] = found[k * size : (k + 1) * size]

    return pl.pallas_call(
        body,
        grid=(width // tile,),
        in_specs=[
            pl.BlockSpec((rows, depth), lambda j: (0, 0)),
            pl.BlockSpec((depth, tile), lambda j: (0, j)),
        ],
        out_specs=[pl.BlockSpec((size, tile), lambda j: (0, j))] * pieces,
        out_shape=[jax.ShapeDtypeStruct((size, width), jnp.float32)] * pieces,
        compiler_params=pltpu.CompilerParams(vmem_limit_bytes=48 << 20),
        cost_estimate=light,
    )(left, weight)


def sum_call(values, group, picks, types, begin=0, width=None):
    rows, full = values[0].shape
    width = full if width is None else width
    tile = max(t for t in range(128, 1793, 128) if width % t == 0 and begin % t == 0)

    def body(*refs):
        total = refs[0][...]
        for one in refs[1 : len(values)]:
            total = total + one[...].astype(jnp.float32)
        for pick, out in zip(picks, refs[len(values) :]):
            held = [total[g * group : (g + 1) * group] for g in pick]
            held = held[0] if len(held) == 1 else jnp.concatenate(held, axis=0)
            out[...] = held.astype(out.dtype)

    return pl.pallas_call(
        body,
        grid=(width // tile,),
        in_specs=[pl.BlockSpec((rows, tile), lambda j: (0, j + begin // tile))] * len(values),
        out_specs=[pl.BlockSpec((group * len(pick), tile), lambda j: (0, j)) for pick in picks],
        out_shape=[
            jax.ShapeDtypeStruct((group * len(pick), width), t) for pick, t in zip(picks, types)
        ],
        compiler_params=pltpu.CompilerParams(vmem_limit_bytes=48 << 20),
        cost_estimate=light,
    )(*values)


def join_call(parts):
    heights = [one.shape[0] for one in parts]
    width = parts[0].shape[1]
    tile = max(t for t in range(128, 2689, 128) if width % t == 0)

    def body(*refs):
        held = [one[...].astype(jnp.float32) for one in refs[:-1]]
        refs[-1][...] = jnp.concatenate(held, axis=0).astype(refs[-1].dtype)

    return pl.pallas_call(
        body,
        grid=(width // tile,),
        in_specs=[pl.BlockSpec((h, tile), lambda j: (0, j)) for h in heights],
        out_specs=pl.BlockSpec((sum(heights), tile), lambda j: (0, j)),
        out_shape=jax.ShapeDtypeStruct((sum(heights), width), parts[0].dtype),
        compiler_params=pltpu.CompilerParams(vmem_limit_bytes=48 << 20),
        cost_estimate=light,
    )(*parts)


def logits_call(parts, weight):
    height = parts[0].shape[0]
    slab, width = weight.shape
    tile = max(t for t in range(128, 1793, 128) if width % t == 0)

    def body(*refs):
        *ins, weight_ref, out = refs

        @pl.when(pl.program_id(0) == 0)
        def _():
            out[...] = jnp.zeros_like(out)

        for k, one in enumerate(ins):
            out[k * height : (k + 1) * height, :] += lax.dot_general(
                one[...], weight_ref[...], (((1,), (1,)), ((), ())),
                preferred_element_type=jnp.float32,
            )

    return pl.pallas_call(
        body,
        grid=(width // tile,),
        in_specs=[pl.BlockSpec((height, tile), lambda j: (0, j))] * len(parts)
        + [pl.BlockSpec((slab, tile), lambda j: (0, j))],
        out_specs=pl.BlockSpec((height * len(parts), slab), lambda j: (0, 0)),
        out_shape=jax.ShapeDtypeStruct((height * len(parts), slab), jnp.float32),
        compiler_params=pltpu.CompilerParams(vmem_limit_bytes=48 << 20),
        cost_estimate=light,
    )(*parts, weight)


def flatten(block):
    owners, depth, columns = block.shape
    return block.astype(jnp.float32).reshape(owners * depth, columns)


def finish_specs(turned, rows, arrived, tile, begin):
    return [
        pl.BlockSpec(turned.shape, lambda j: (0, 0)),
        pl.BlockSpec((rows.shape[0], tile), lambda j: (0, j + begin)),
        pl.BlockSpec(arrived.shape[:2] + (tile,), lambda j: (0, 0, j)),
    ]


def finish_tile(scale, turned_ref, rows_ref, arrived_ref, hot):
    head = jnp.dot(turned_ref[...], rows_ref[...], preferred_element_type=jnp.float32)
    flat = flatten(arrived_ref[...]).astype(jnp.bfloat16)
    embed = jnp.dot(hot, flat, preferred_element_type=jnp.float32)
    return (head + scale * embed).astype(jnp.bfloat16)


def begin_call(turned, rows, arrived, tile, count, tag_at):
    width = rows.shape[1]
    slab = turned.shape[0]
    slots = arrived.shape[0] * arrived.shape[1]

    def body(turned_ref, rows_ref, arrived_ref, tag_ref, out_ref, hot_ref):
        @pl.when(pl.program_id(0) == 0)
        def _():
            tags = flatten(tag_ref[...]).T
            ids = (tags[0:1] - 1.0) * 256.0 + tags[1:2]
            row = lax.broadcasted_iota(jnp.int32, (slab, slots), 0).astype(jnp.float32)
            hot_ref[...] = jnp.where(row == ids, 1.0, 0.0).astype(jnp.bfloat16)

        out_ref[...] = finish_tile(
            math.sqrt(width), turned_ref, rows_ref, arrived_ref, hot_ref[...]
        )

    return pl.pallas_call(
        body,
        grid=(count,),
        in_specs=finish_specs(turned, rows, arrived, tile, 0)
        + [pl.BlockSpec(arrived.shape[:2] + (128,), lambda j: (0, 0, tag_at // 128))],
        out_specs=[
            pl.BlockSpec((slab, tile), lambda j: (0, j)),
            pl.BlockSpec((slab, slots), lambda j: (0, 0)),
        ],
        out_shape=[
            jax.ShapeDtypeStruct((slab, width), jnp.bfloat16),
            jax.ShapeDtypeStruct((slab, slots), jnp.bfloat16),
        ],
        compiler_params=pltpu.CompilerParams(vmem_limit_bytes=48 << 20),
        cost_estimate=light,
    )(turned, rows, arrived, arrived)


def finish_call(turned, rows, arrived, hot, begun, tile, begin, count):
    width = rows.shape[1]
    slab, slots = hot.shape

    def body(turned_ref, rows_ref, arrived_ref, hot_ref, begun_ref, out_ref):
        out_ref[...] = finish_tile(
            math.sqrt(width), turned_ref, rows_ref, arrived_ref, hot_ref[...]
        )

    return pl.pallas_call(
        body,
        grid=(count,),
        in_specs=finish_specs(turned, rows, arrived, tile, begin)
        + [pl.BlockSpec((slab, slots), lambda j: (0, 0)), pl.BlockSpec(memory_space=pl.ANY)],
        out_specs=pl.BlockSpec((slab, tile), lambda j: (0, j + begin)),
        out_shape=jax.ShapeDtypeStruct((slab, width), jnp.bfloat16),
        input_output_aliases={4: 0},
        compiler_params=pltpu.CompilerParams(vmem_limit_bytes=48 << 20),
        cost_estimate=light,
    )(turned, rows, arrived, hot, begun)


def shards(
    weight, hidden, targets, branch, pair_of_row, ref_log_prob, pair_weight, token_ids, token_grad
):
    vocab_rows, model_width = weight.shape
    owned = hidden.shape[0]
    x, y, core, z = (lax.axis_index(a) for a in ("x", "y", "core", "tensor"))
    nx, ny, nc, nz = (lax.axis_size(a) for a in ("x", "y", "core", "tensor"))
    owners = nx * ny * nc * nz
    me = ((x * ny + y) * nc + core) * nz + z
    vocab_start = me * vocab_rows
    every = ("x", "y", "core", "tensor")

    token_count = token_ids.shape[0]
    capacity = max(2, (2 * token_count + owners - 1) // owners)
    row_owner = token_ids // vocab_rows
    local = token_ids - row_owner * vocab_rows
    position = jnp.arange(token_count, dtype=jnp.int32)
    earlier = (row_owner[:, None] == row_owner[None, :]) & (position[None, :] < position[:, None])
    slot = jnp.sum(earlier.astype(jnp.int32), axis=1)
    pick = (
        jnp.arange(owners * capacity, dtype=jnp.int32)[:, None]
        == (row_owner * capacity + slot)[None, :]
    ).astype(jnp.bfloat16)
    lane = jnp.arange(128, dtype=jnp.int32)[None, :]
    tag = jnp.where(
        lane == 0, (local // 256 + 1)[:, None], jnp.where(lane == 1, (local % 256)[:, None], 0)
    )
    half = model_width // 256 * 128
    first_part = jnp.concatenate([token_grad[:, :half], tag.astype(jnp.bfloat16)], axis=1)
    second_part = token_grad[:, half:]

    out_first = spread_call(pick, first_part, capacity)
    out_second = spread_call(pick, second_part, capacity)
    rows = join_call([hidden] + others(hidden, "x"))
    rows, out_first = lax.optimization_barrier((rows, out_first))
    arrived_first = lax.all_to_all(out_first, every, 0, 0, tiled=True)
    came = others(rows, "y")
    *came, out_second = lax.optimization_barrier((*came, out_second))
    rows = join_call([rows] + came)
    halves = [rows, shift(rows, "core", 1)]
    gathered = jnp.concatenate(halves, axis=0)
    step_y, step_x = jnp.meshgrid(jnp.arange(ny), jnp.arange(nx), indexing="ij")
    plane = ((x - step_x + nx) % nx * ny + (y - step_y + ny) % ny).reshape(-1)
    block_of = jnp.concatenate([plane * nc + core, plane * nc + (core + 1) % nc])
    row_of = (block_of[:, None] * owned + jnp.arange(owned)[None, :]).reshape(-1)

    logits = logits_call(halves, weight)
    place = row_of[:, None] == jnp.arange(row_of.shape[0])[None, :]

    def take(v):
        return jnp.sum(jnp.where(place, v[None, :], 0), axis=1)

    def untake(v):
        return jnp.sum(jnp.where(place, v[:, None], 0), axis=0)

    columns = jnp.arange(vocab_rows, dtype=jnp.int32)
    target_hit = (columns[None, :] == (take(targets) - vocab_start)[:, None]).astype(jnp.float32)
    target_part = jnp.sum(logits * target_hit, axis=1)
    top_part = jnp.max(logits, axis=1)
    total_part = jnp.sum(jnp.exp(logits - top_part[:, None]), axis=1)
    stats = jnp.stack([untake(top_part), untake(total_part), untake(target_part)])
    def merge(both):
        top = both[0][0]
        for one in both[1:]:
            top = jnp.maximum(top, one[0])
        total = sum(one[1] * jnp.exp(one[0] - top) for one in both)
        return jnp.stack([top, total, sum(one[2] for one in both)])

    for axis in ("core", "y", "x"):
        stats = merge([stats] + others(stats, axis))
    for step in (1, 2, 4):
        stats = merge([stats, shift(stats, "tensor", step)])
    stats, arrived_first, out_second = lax.optimization_barrier((stats, arrived_first, out_second))
    arrived_second = lax.all_to_all(out_second, every, 0, 0, tiled=True)
    row_top, row_total, target_logit = stats[0], stats[1], stats[2]
    log_prob = target_logit - row_top - jnp.log(row_total)
    branch_sign = (branch == 1).astype(jnp.float32) - (branch == 2).astype(jnp.float32)
    pair_count = pair_weight.shape[0]
    member = (pair_of_row[:, None] == jnp.arange(pair_count, dtype=jnp.int32)[None, :]).astype(
        jnp.float32
    )
    margin = jnp.sum(member * (branch_sign * (log_prob - ref_log_prob))[:, None], axis=0)
    dpo_loss = jnp.sum(pair_weight * jax.nn.softplus(-dpo_beta * margin))
    push_back = pair_weight * jax.nn.sigmoid(-dpo_beta * margin)
    row_scale = -dpo_beta * branch_sign * jnp.sum(member * push_back[None, :], axis=1)
    probs = jnp.exp(logits - take(row_top)[:, None]) / take(row_total)[:, None]
    dlogits = (take(row_scale)[:, None] * (target_hit - probs)).astype(jnp.bfloat16)

    narrow, wide = jnp.bfloat16, jnp.float32
    own, away = product_call(dlogits, weight, nc)
    both = [own, shift(away, "core", nc - 1)]
    columns_each = model_width // 2

    def reduce_along(values, axis, group, picks, types):
        size = lax.axis_size(axis)
        came = [shift(values[step], axis, size - step) for step in range(1, size)]
        return sum_call([values[0]] + came, group, picks, types)

    by_y = [[i * nx + j for j in range(nx)] for i in range(ny)]
    by_x = [[i * nx + j for i in range(ny)] for j in range(nx)]
    side_y = sum_call(both, owned, by_y, [wide] + [narrow] * (ny - 1), 0, columns_each)
    side_x = sum_call(both, owned, by_x, [wide] + [narrow] * (nx - 1), columns_each, columns_each)
    side_y = reduce_along(side_y, "y", owned, [[j] for j in range(nx)], [wide] * nx)
    side_x = reduce_along(side_x, "x", owned, [[i] for i in range(ny)], [wide] * ny)
    side_y = reduce_along(side_y, "x", owned, [[0]], [wide])[0]
    side_x = reduce_along(side_x, "y", owned, [[0]], [wide])[0]
    part = jnp.concatenate([side_y, side_x], axis=1)
    sent = part.astype(narrow)

    turned = dlogits.T
    tile = max(
        t for t in range(128, 897, 128) if half % t == 0 and (model_width - half) % t == 0
    )
    begun, hot = begin_call(turned, gathered, arrived_first, tile, half // tile, half)
    sent, begun = lax.optimization_barrier((sent, begun))
    near = [shift(sent, "tensor", 1), shift(sent, "tensor", nz - 1)]
    *near, arrived_second = lax.optimization_barrier((*near, arrived_second))
    hidden_grad = part + sum(o.astype(jnp.float32) for o in round_ring(near, "tensor"))
    hidden_grad = hidden_grad.astype(jnp.bfloat16)

    weight_grad = finish_call(
        turned, gathered, arrived_second, hot, begun, tile, half // tile,
        (model_width - half) // tile,
    )
    return (dpo_loss, weight_grad, hidden_grad)


def solution(mesh):
    fine = Mesh(mesh.devices.reshape(4, 4, 2, 8), ("x", "y", "core", "tensor"))
    seq = ("x", "y", "core")
    every = ("x", "y", "core", "tensor")
    return jax.shard_map(
        shards,
        mesh=fine,
        in_specs=(P(every, None), P(seq, None), P(), P(), P(), P(), P(), P(every), P(every, None)),
        out_specs=(P(), P(every, None), P(seq, None)),
        check_vma=False,
    )
```

```python
import math

import jax
import jax.numpy as jnp
from jax import lax
from jax.experimental import pallas as pl
from jax.experimental.pallas import tpu as pltpu
from jax.sharding import Mesh
from jax.sharding import PartitionSpec as P

dpo_beta = 0.1


def shift(value, axis, step):
    size = lax.axis_size(axis)
    return lax.ppermute(value, axis, [(i, (i + step) % size) for i in range(size)])


def others(value, axis):
    return [shift(value, axis, step) for step in range(1, lax.axis_size(axis))]


light = pl.CostEstimate(flops=0, bytes_accessed=0, transcendentals=0)


def spread_call(matrix, rows, depth):
    places, count = matrix.shape
    width = rows.shape[1]
    tile = max(t for t in range(128, 1409, 128) if width % t == 0)

    def body(matrix_ref, rows_ref, out_ref):
        found = jnp.dot(matrix_ref[...], rows_ref[...], preferred_element_type=jnp.float32)
        out_ref[...] = found.reshape(places // depth, depth, tile).astype(out_ref.dtype)

    return pl.pallas_call(
        body,
        grid=(width // tile,),
        in_specs=[
            pl.BlockSpec((places, count), lambda j: (0, 0)),
            pl.BlockSpec((count, tile), lambda j: (0, j)),
        ],
        out_specs=pl.BlockSpec((places // depth, depth, tile), lambda j: (0, 0, j)),
        out_shape=jax.ShapeDtypeStruct((places // depth, depth, width), jnp.bfloat16),
        compiler_params=pltpu.CompilerParams(vmem_limit_bytes=48 << 20),
        cost_estimate=light,
    )(matrix, rows)


def product_call(left, weight, pieces):
    rows, depth = left.shape
    width = weight.shape[1]
    tile = max(t for t in range(128, 1793, 128) if width % t == 0)
    size = rows // pieces

    def body(left_ref, weight_ref, *outs):
        found = jnp.dot(left_ref[...], weight_ref[...], preferred_element_type=jnp.float32)
        for k, out in enumerate(outs):
            out[...] = found[k * size : (k + 1) * size]

    return pl.pallas_call(
        body,
        grid=(width // tile,),
        in_specs=[
            pl.BlockSpec((rows, depth), lambda j: (0, 0)),
            pl.BlockSpec((depth, tile), lambda j: (0, j)),
        ],
        out_specs=[pl.BlockSpec((size, tile), lambda j: (0, j))] * pieces,
        out_shape=[jax.ShapeDtypeStruct((size, width), jnp.float32)] * pieces,
        compiler_params=pltpu.CompilerParams(vmem_limit_bytes=48 << 20),
        cost_estimate=light,
    )(left, weight)


def sum_call(values, group, picks, types, begin=0, width=None):
    rows, full = values[0].shape
    width = full if width is None else width
    tile = max(t for t in range(128, 1793, 128) if width % t == 0 and begin % t == 0)

    def body(*refs):
        total = refs[0][...]
        for one in refs[1 : len(values)]:
            total = total + one[...].astype(jnp.float32)
        for pick, out in zip(picks, refs[len(values) :]):
            held = [total[g * group : (g + 1) * group] for g in pick]
            held = held[0] if len(held) == 1 else jnp.concatenate(held, axis=0)
            out[...] = held.astype(out.dtype)

    return pl.pallas_call(
        body,
        grid=(width // tile,),
        in_specs=[pl.BlockSpec((rows, tile), lambda j: (0, j + begin // tile))] * len(values),
        out_specs=[pl.BlockSpec((group * len(pick), tile), lambda j: (0, j)) for pick in picks],
        out_shape=[
            jax.ShapeDtypeStruct((group * len(pick), width), t) for pick, t in zip(picks, types)
        ],
        compiler_params=pltpu.CompilerParams(vmem_limit_bytes=48 << 20),
        cost_estimate=light,
    )(*values)


def join_call(parts):
    heights = [one.shape[0] for one in parts]
    width = parts[0].shape[1]
    tile = max(t for t in range(128, 2689, 128) if width % t == 0)

    def body(*refs):
        held = [one[...].astype(jnp.float32) for one in refs[:-1]]
        refs[-1][...] = jnp.concatenate(held, axis=0).astype(refs[-1].dtype)

    return pl.pallas_call(
        body,
        grid=(width // tile,),
        in_specs=[pl.BlockSpec((h, tile), lambda j: (0, j)) for h in heights],
        out_specs=pl.BlockSpec((sum(heights), tile), lambda j: (0, j)),
        out_shape=jax.ShapeDtypeStruct((sum(heights), width), parts[0].dtype),
        compiler_params=pltpu.CompilerParams(vmem_limit_bytes=48 << 20),
        cost_estimate=light,
    )(*parts)


def logits_call(parts, weight):
    height = parts[0].shape[0]
    slab, width = weight.shape
    tile = max(t for t in range(128, 1793, 128) if width % t == 0)

    def body(*refs):
        *ins, weight_ref, out = refs

        @pl.when(pl.program_id(0) == 0)
        def _():
            out[...] = jnp.zeros_like(out)

        for k, one in enumerate(ins):
            out[k * height : (k + 1) * height, :] += lax.dot_general(
                one[...], weight_ref[...], (((1,), (1,)), ((), ())),
                preferred_element_type=jnp.float32,
            )

    return pl.pallas_call(
        body,
        grid=(width // tile,),
        in_specs=[pl.BlockSpec((height, tile), lambda j: (0, j))] * len(parts)
        + [pl.BlockSpec((slab, tile), lambda j: (0, j))],
        out_specs=pl.BlockSpec((height * len(parts), slab), lambda j: (0, 0)),
        out_shape=jax.ShapeDtypeStruct((height * len(parts), slab), jnp.float32),
        compiler_params=pltpu.CompilerParams(vmem_limit_bytes=48 << 20),
        cost_estimate=light,
    )(*parts, weight)


def flatten(block):
    owners, depth, columns = block.shape
    return block.astype(jnp.float32).reshape(owners * depth, columns)


def finish_specs(turned, rows, arrived, tile, begin):
    return [
        pl.BlockSpec(turned.shape, lambda j: (0, 0)),
        pl.BlockSpec((rows.shape[0], tile), lambda j: (0, j + begin)),
        pl.BlockSpec(arrived.shape[:2] + (tile,), lambda j: (0, 0, j)),
    ]


def finish_tile(scale, turned_ref, rows_ref, arrived_ref, hot):
    head = jnp.dot(turned_ref[...], rows_ref[...], preferred_element_type=jnp.float32)
    flat = flatten(arrived_ref[...]).astype(jnp.bfloat16)
    embed = jnp.dot(hot, flat, preferred_element_type=jnp.float32)
    return (head + scale * embed).astype(jnp.bfloat16)


def begin_call(turned, rows, arrived, tile, count, tag_at):
    width = rows.shape[1]
    slab = turned.shape[0]
    slots = arrived.shape[0] * arrived.shape[1]

    def body(turned_ref, rows_ref, arrived_ref, tag_ref, out_ref, hot_ref):
        @pl.when(pl.program_id(0) == 0)
        def _():
            tags = flatten(tag_ref[...]).T
            ids = (tags[0:1] - 1.0) * 256.0 + tags[1:2]
            row = lax.broadcasted_iota(jnp.int32, (slab, slots), 0).astype(jnp.float32)
            hot_ref[...] = jnp.where(row == ids, 1.0, 0.0).astype(jnp.bfloat16)

        out_ref[...] = finish_tile(
            math.sqrt(width), turned_ref, rows_ref, arrived_ref, hot_ref[...]
        )

    return pl.pallas_call(
        body,
        grid=(count,),
        in_specs=finish_specs(turned, rows, arrived, tile, 0)
        + [pl.BlockSpec(arrived.shape[:2] + (128,), lambda j: (0, 0, tag_at // 128))],
        out_specs=[
            pl.BlockSpec((slab, tile), lambda j: (0, j)),
            pl.BlockSpec((slab, slots), lambda j: (0, 0)),
        ],
        out_shape=[
            jax.ShapeDtypeStruct((slab, width), jnp.bfloat16),
            jax.ShapeDtypeStruct((slab, slots), jnp.bfloat16),
        ],
        compiler_params=pltpu.CompilerParams(vmem_limit_bytes=48 << 20),
        cost_estimate=light,
    )(turned, rows, arrived, arrived)


def finish_call(turned, rows, arrived, hot, begun, tile, begin, count):
    width = rows.shape[1]
    slab, slots = hot.shape

    def body(turned_ref, rows_ref, arrived_ref, hot_ref, begun_ref, out_ref):
        out_ref[...] = finish_tile(
            math.sqrt(width), turned_ref, rows_ref, arrived_ref, hot_ref[...]
        )

    return pl.pallas_call(
        body,
        grid=(count,),
        in_specs=finish_specs(turned, rows, arrived, tile, begin)
        + [pl.BlockSpec((slab, slots), lambda j: (0, 0)), pl.BlockSpec(memory_space=pl.ANY)],
        out_specs=pl.BlockSpec((slab, tile), lambda j: (0, j + begin)),
        out_shape=jax.ShapeDtypeStruct((slab, width), jnp.bfloat16),
        input_output_aliases={4: 0},
        compiler_params=pltpu.CompilerParams(vmem_limit_bytes=48 << 20),
        cost_estimate=light,
    )(turned, rows, arrived, hot, begun)


def shards(
    weight, hidden, targets, branch, pair_of_row, ref_log_prob, pair_weight, token_ids, token_grad
):
    vocab_rows, model_width = weight.shape
    owned = hidden.shape[0]
    x, y, core, z = (lax.axis_index(a) for a in ("x", "y", "core", "tensor"))
    nx, ny, nc, nz = (lax.axis_size(a) for a in ("x", "y", "core", "tensor"))
    owners = nx * ny * nc * nz
    me = ((x * ny + y) * nc + core) * nz + z
    vocab_start = me * vocab_rows
    every = ("x", "y", "core", "tensor")

    token_count = token_ids.shape[0]
    capacity = max(2, (2 * token_count + owners - 1) // owners)
    row_owner = token_ids // vocab_rows
    local = token_ids - row_owner * vocab_rows
    position = jnp.arange(token_count, dtype=jnp.int32)
    earlier = (row_owner[:, None] == row_owner[None, :]) & (position[None, :] < position[:, None])
    slot = jnp.sum(earlier.astype(jnp.int32), axis=1)
    pick = (
        jnp.arange(owners * capacity, dtype=jnp.int32)[:, None]
        == (row_owner * capacity + slot)[None, :]
    ).astype(jnp.bfloat16)
    lane = jnp.arange(128, dtype=jnp.int32)[None, :]
    tag = jnp.where(
        lane == 0, (local // 256 + 1)[:, None], jnp.where(lane == 1, (local % 256)[:, None], 0)
    )
    half = model_width // 256 * 128
    first_part = jnp.concatenate([token_grad[:, :half], tag.astype(jnp.bfloat16)], axis=1)
    second_part = token_grad[:, half:]

    out_first = spread_call(pick, first_part, capacity)
    out_second = spread_call(pick, second_part, capacity)
    rows = join_call([hidden] + others(hidden, "x"))
    rows, out_first = lax.optimization_barrier((rows, out_first))
    arrived_first = lax.all_to_all(out_first, every, 0, 0, tiled=True)
    came = others(rows, "y")
    *came, out_second = lax.optimization_barrier((*came, out_second))
    rows = join_call([rows] + came)
    halves = [rows, shift(rows, "core", 1)]
    gathered = jnp.concatenate(halves, axis=0)
    step_y, step_x = jnp.meshgrid(jnp.arange(ny), jnp.arange(nx), indexing="ij")
    plane = ((x - step_x + nx) % nx * ny + (y - step_y + ny) % ny).reshape(-1)
    block_of = jnp.concatenate([plane * nc + core, plane * nc + (core + 1) % nc])
    row_of = (block_of[:, None] * owned + jnp.arange(owned)[None, :]).reshape(-1)

    logits = logits_call(halves, weight)
    place = row_of[:, None] == jnp.arange(row_of.shape[0])[None, :]

    def take(v):
        return jnp.sum(jnp.where(place, v[None, :], 0), axis=1)

    def untake(v):
        return jnp.sum(jnp.where(place, v[:, None], 0), axis=0)

    columns = jnp.arange(vocab_rows, dtype=jnp.int32)
    target_hit = (columns[None, :] == (take(targets) - vocab_start)[:, None]).astype(jnp.float32)
    target_part = jnp.sum(logits * target_hit, axis=1)
    top_part = jnp.max(logits, axis=1)
    total_part = jnp.sum(jnp.exp(logits - top_part[:, None]), axis=1)
    stats = jnp.stack([untake(top_part), untake(total_part), untake(target_part)])
    def merge(both):
        top = both[0][0]
        for one in both[1:]:
            top = jnp.maximum(top, one[0])
        total = sum(one[1] * jnp.exp(one[0] - top) for one in both)
        return jnp.stack([top, total, sum(one[2] for one in both)])

    for axis in ("core", "y", "x"):
        stats = merge([stats] + others(stats, axis))
    for step in (4, 2, 1):
        stats = merge([stats, shift(stats, "tensor", step)])
    stats, arrived_first, out_second = lax.optimization_barrier((stats, arrived_first, out_second))
    arrived_second = lax.all_to_all(out_second, every, 0, 0, tiled=True)
    row_top, row_total, target_logit = stats[0], stats[1], stats[2]
    log_prob = target_logit - row_top - jnp.log(row_total)
    branch_sign = (branch == 1).astype(jnp.float32) - (branch == 2).astype(jnp.float32)
    pair_count = pair_weight.shape[0]
    member = (pair_of_row[:, None] == jnp.arange(pair_count, dtype=jnp.int32)[None, :]).astype(
        jnp.float32
    )
    margin = jnp.sum(member * (branch_sign * (log_prob - ref_log_prob))[:, None], axis=0)
    dpo_loss = jnp.sum(pair_weight * jax.nn.softplus(-dpo_beta * margin))
    push_back = pair_weight * jax.nn.sigmoid(-dpo_beta * margin)
    row_scale = -dpo_beta * branch_sign * jnp.sum(member * push_back[None, :], axis=1)
    probs = jnp.exp(logits - take(row_top)[:, None]) / take(row_total)[:, None]
    dlogits = (take(row_scale)[:, None] * (target_hit - probs)).astype(jnp.bfloat16)

    narrow, wide = jnp.bfloat16, jnp.float32
    own, away = product_call(dlogits, weight, nc)
    both = [own, shift(away, "core", nc - 1)]
    columns_each = model_width // 2

    def reduce_along(values, axis, group, picks, types):
        size = lax.axis_size(axis)
        came = [shift(values[step], axis, size - step) for step in range(1, size)]
        return sum_call([values[0]] + came, group, picks, types)

    by_y = [[i * nx + j for j in range(nx)] for i in range(ny)]
    by_x = [[i * nx + j for i in range(ny)] for j in range(nx)]
    side_y = sum_call(both, owned, by_y, [wide] + [narrow] * (ny - 1), 0, columns_each)
    side_x = sum_call(both, owned, by_x, [wide] + [narrow] * (nx - 1), columns_each, columns_each)
    side_y = reduce_along(side_y, "y", owned, [[j] for j in range(nx)], [wide] * nx)
    side_x = reduce_along(side_x, "x", owned, [[i] for i in range(ny)], [wide] * ny)
    side_y = reduce_along(side_y, "x", owned, [[0]], [wide])[0]
    side_x = reduce_along(side_x, "y", owned, [[0]], [wide])[0]
    part = jnp.concatenate([side_y, side_x], axis=1)
    sent = part.astype(narrow)

    turned = dlogits.T
    tile = max(
        t for t in range(128, 897, 128) if half % t == 0 and (model_width - half) % t == 0
    )
    begun, hot = begin_call(turned, gathered, arrived_first, tile, half // tile, half)
    sent, begun = lax.optimization_barrier((sent, begun))
    near = [shift(sent, "tensor", step) for step in (1, nz - 1, 2, nz - 2)]
    *near, arrived_second = lax.optimization_barrier((*near, arrived_second))
    far = [shift(near[2], "tensor", 1), shift(near[3], "tensor", nz - 1), shift(near[2], "tensor", 2)]
    hidden_grad = part + sum(o.astype(jnp.float32) for o in near + far)
    hidden_grad = hidden_grad.astype(jnp.bfloat16)

    weight_grad = finish_call(
        turned, gathered, arrived_second, hot, begun, tile, half // tile,
        (model_width - half) // tile,
    )
    return (dpo_loss, weight_grad, hidden_grad)


def solution(mesh):
    fine = Mesh(mesh.devices.reshape(4, 4, 2, 8), ("x", "y", "core", "tensor"))
    seq = ("x", "y", "core")
    every = ("x", "y", "core", "tensor")
    return jax.shard_map(
        shards,
        mesh=fine,
        in_specs=(P(every, None), P(seq, None), P(), P(), P(), P(), P(), P(every), P(every, None)),
        out_specs=(P(), P(every, None), P(seq, None)),
        check_vma=False,
    )
```
